1024 devices in a mesh: narrow: 16 (over x, y_lo), wide: 64 (over z, y_hi, core).
Axes of the slice: x: 4, y: 8 (y_hi: 2, y_lo: 4; y = y_hi * 4 + y_lo), z: 16, core: 2. Of those that a mesh axis runs over, the one named last changes fastest.
Arguments:
- amplitudes: float32 [16, 64, 2, 2, 256, 256], P('narrow', 'wide'), may hold values from -6 to 6
- first_gate: float32 [2, 256, 256], replicated, may hold values from -0.25 to 0.25
- second_gate: float32 [2, 256, 256], replicated, may hold values from -0.25 to 0.25
- swap_gates: float32 [2, 2, 256, 256], replicated, may hold values from -0.25 to 0.25
Outputs:
- final_state: float32 [16, 64, 2, 2, 256, 256], P('narrow', 'wide')
The draws below stay inside these ranges and needn't reach their ends.
All inputs are finite; a program needn't handle non-finite values.
Results may differ from the reference program's by a relative error of at most 0.00007.
Values sent between devices are 32-bit elements; how exact they have to be, the bound alone decides.
A program may use at most 32 MiB of HBM per device.

```python
import jax
import jax.numpy as jnp
from jax import lax

REG = 256
EXTRA = 2
SWAPS = 2
NARROWS = 16
WIDES = 64
N_NARROW = 16
N_WIDE = 64


def shard_levels(own_key, shape, cuts, smallest, top_value):
    def one(position, parts):
        draws = jax.random.uniform(jax.random.fold_in(jax.random.fold_in(own_key, 6), position), (parts,), jnp.float32, smallest / len(cuts), top_value / len(cuts))
        return jnp.repeat(jnp.exp(draws), shape[position] // parts).reshape((-1,) + (1,) * (len(shape) - position - 1))

    factor_of = one(*cuts[0])
    for cut in cuts[1:]:
        factor_of = factor_of * one(*cut)
    return factor_of


def normal_values(rng, dims, width, most, cuts=(), kind=jnp.bfloat16):
    level = shard_levels(rng, dims, cuts, -0.22, 0.18) if cuts else 1.0
    entries = jax.random.normal(rng, dims, jnp.float32) * width * level
    return jnp.minimum(jnp.maximum(entries, -most), most).astype(kind)


def setup_inputs(seed: int = 0) -> dict:
    streams_of = jax.random.split(jax.random.key(seed), 5)
    return {
        "amplitudes": normal_values(streams_of[0], (NARROWS, WIDES, 2, EXTRA, REG, REG), 1.0, 6.0, ((0, 16), (1, 64)), jnp.float32),
        "first_gate": normal_values(streams_of[1], (2, REG, REG), (2 * REG) ** -0.5, 0.25, (), jnp.float32),
        "second_gate": normal_values(streams_of[2], (2, REG, REG), (2 * REG) ** -0.5, 0.25, (), jnp.float32),
        "swap_gates": normal_values(streams_of[3], (SWAPS, 2, REG, REG), (2 * REG) ** -0.5, 0.25, (), jnp.float32),
    }


def mixing(matrix, values, form):
    return jnp.einsum(form, matrix, values, precision=lax.Precision.HIGHEST)


def turn_rows(gate, field):
    real = field[:, :, 0]
    imag = field[:, :, 1]
    form = "ij,nwcjb->nwcib"
    out_real = mixing(gate[0], real, form) - mixing(gate[1], imag, form)
    out_imag = mixing(gate[0], imag, form) + mixing(gate[1], real, form)
    return jnp.stack([out_real, out_imag], axis=2)


def turn_columns(gate, field):
    real = field[:, :, 0]
    imag = field[:, :, 1]
    form = "ij,nwcaj->nwcai"
    out_real = mixing(gate[0], real, form) - mixing(gate[1], imag, form)
    out_imag = mixing(gate[0], imag, form) + mixing(gate[1], real, form)
    return jnp.stack([out_real, out_imag], axis=2)


def each_slab(action, gate, field):
    def inner(one_slab):
        return action(gate, one_slab[None])[0]
    return lax.map(inner, field)


def swap_narrow(field, bit):
    shape = field.shape
    reshaped = field.reshape(shape[0] >> (bit + 1), 2, 1 << bit, shape[1], 2, shape[3], 2, shape[4] // 2, shape[5])
    return jnp.swapaxes(reshaped, 1, 6).reshape(shape)


def regroup(field):
    shape = field.shape
    reshaped = field.reshape(shape[0], shape[1], 2, shape[3], shape[4], N_WIDE, shape[5] // N_WIDE)
    return jnp.swapaxes(reshaped, 1, 5).reshape(shape)


def reference(amplitudes, first_gate, second_gate, swap_gates):
    state = each_slab(turn_rows, first_gate, amplitudes)
    state = each_slab(turn_columns, second_gate, state)
    state = swap_narrow(state, 0)
    state = each_slab(turn_rows, swap_gates[0], state)
    state = swap_narrow(state, N_NARROW.bit_length() - 2)
    state = each_slab(turn_rows, swap_gates[1], state)
    return regroup(state)
```

```python
import functools

import jax
import jax.numpy as jnp
from jax import lax
from jax.experimental import pallas as pl
from jax.experimental.pallas import tpu as pltpu
from jax.sharding import PartitionSpec as P

MESH = pl.DeviceIdType.MESH
F32 = jnp.float32
BF16 = jnp.bfloat16
NN = (((1,), (0,)), ((), ()))
NT = (((1,), (1,)), ((), ()))


def split(x):
    high = x.astype(BF16)
    return high, (x - high.astype(F32)).astype(BF16)


def product(left, right, dims):
    dot = functools.partial(lax.dot_general, dimension_numbers=dims, preferred_element_type=F32)
    return dot(left[0], right[0]) + (dot(left[0], right[1]) + dot(left[1], right[0]))


def complex_product(left, right, dims):
    real = product(left[0], right[0], dims) - product(left[1], right[1], dims)
    imag = product(left[0], right[1], dims) + product(left[1], right[0], dims)
    return real, imag


def top_rows(shape):
    return lax.broadcasted_iota(jnp.int32, shape, 1) < 4


def interleave(real, imag):
    a = real.reshape(-1, 8, real.shape[-1])
    b = imag.reshape(-1, 8, imag.shape[-1])
    top = top_rows(a.shape)
    even = jnp.where(top, a, pltpu.roll(b, 4, 1))
    odd = jnp.where(top, pltpu.roll(a, 4, 1), b)
    return jnp.stack([even, odd], axis=1).reshape(-1, real.shape[-1])


def deinterleave(both):
    pairs = both.reshape(-1, 2, 8, both.shape[-1])
    even, odd = pairs[:, 0], pairs[:, 1]
    top = top_rows(even.shape)
    real = jnp.where(top, even, pltpu.roll(odd, 4, 1))
    imag = jnp.where(top, pltpu.roll(even, 4, 1), odd)
    return real.reshape(-1, both.shape[-1]), imag.reshape(-1, both.shape[-1])


def kernel(n_narrow, n_wide, x_hbm, g1_hbm, g2_hbm, gs_hbm, out_hbm,
           x, gates, split_gates, send_a, state_a, send_b, state_b, turned0, got0,
           turned1, got1, tsend_a, tstate_a, tsend_b, tstate_b, result,
           in_sem, out_sem, swap_send, swap_recv, group_send, group_recv):
    n = lax.axis_index("narrow")
    w = lax.axis_index("wide")
    reg = x.shape[-1]
    half = reg // 2
    top_bit = n_narrow.bit_length() - 2
    bits = (lax.rem(n, 2), lax.rem(n // 2**top_bit, 2))
    partners = (n + 1 - 2 * bits[0], n + (1 - 2 * bits[1]) * 2**top_bit)

    loads = [
        pltpu.make_async_copy(g1_hbm, gates.at[0], in_sem.at[0]),
        pltpu.make_async_copy(x_hbm.at[:, 0], x.at[:, 0], in_sem.at[1]),
        pltpu.make_async_copy(g2_hbm, gates.at[1], in_sem.at[2]),
        pltpu.make_async_copy(x_hbm.at[:, 1], x.at[:, 1], in_sem.at[3]),
        pltpu.make_async_copy(gs_hbm.at[0], gates.at[2], in_sem.at[4]),
        pltpu.make_async_copy(gs_hbm.at[1], gates.at[3], in_sem.at[5]),
    ]
    for load in loads:
        load.start()

    barrier = pltpu.get_barrier_semaphore()
    for partner in partners:
        pl.semaphore_signal(barrier, inc=1, device_id=(partner, w), device_id_type=MESH)

    @pl.loop(1, n_wide)
    def _(k):
        pl.semaphore_signal(barrier, inc=1, device_id=(n, lax.rem(w + k, n_wide)), device_id_type=MESH)

    def prepare(index):
        for part in range(2):
            split_gates[index, part, 0], split_gates[index, part, 1] = split(gates[index, part])

    def gate(index, rows=slice(None)):
        return [(split_gates[index, part, 0, rows, :], split_gates[index, part, 1, rows, :]) for part in range(2)]

    def swap(number, slot, source, target):
        return pltpu.make_async_remote_copy(
            src_ref=source, dst_ref=target, send_sem=swap_send.at[slot], recv_sem=swap_recv.at[slot],
            device_id=(partners[number], w), device_id_type=MESH)

    def group(slot, source, target):
        @pl.loop(1, n_wide)
        def _(k):
            other = lax.rem(w + k, n_wide)
            pltpu.make_async_remote_copy(
                src_ref=source.at[pl.ds(pl.multiple_of(other * 8, 8), 8)],
                dst_ref=target.at[pl.ds(pl.multiple_of(w * 8, 8), 8)],
                send_sem=group_send.at[slot], recv_sem=group_recv.at[slot],
                device_id=(n, other), device_id_type=MESH).start()
        own = pl.ds(pl.multiple_of(w * 8, 8), 8)
        target[own, :] = source[own, :]

    def group_wait(slot, source, target):
        moved = pl.ds(0, 8 * (n_wide - 1))
        whole = pltpu.make_async_remote_copy(
            src_ref=source.at[moved], dst_ref=target.at[moved],
            send_sem=group_send.at[slot], recv_sem=group_recv.at[slot],
            device_id=(n, lax.rem(w + 1, n_wide)), device_id_type=MESH)
        return whole

    def rows_of(bit):
        return pl.ds(pl.multiple_of(bit * half, half), half)

    def natural_gate(index, number, values, send, state):
        bit = bits[number]
        send[0], send[1] = complex_product(gate(index, rows_of(1 - bit)), values, NN)
        copy = swap(number, number, send, state.at[:, rows_of(bit), :])
        keep = functools.partial(keep_natural, index, bit, values, state)
        return copy, keep

    def keep_natural(index, bit, values, state):
        real, imag = complex_product(gate(index, rows_of(bit)), values, NN)
        state[0, rows_of(bit), :] = real
        state[1, rows_of(bit), :] = imag

    def turned_gate(index, number, values, send, state):
        bit = bits[number]
        send[0], send[1] = complex_product(values, gate(index, rows_of(1 - bit)), NT)
        copy = swap(number, 2 + number, send, state.at[bit])
        keep = functools.partial(keep_turned, index, bit, values, state)
        return copy, keep

    def keep_turned(index, bit, values, state):
        real, imag = complex_product(values, gate(index, rows_of(bit)), NT)
        state[bit, 0] = real
        state[bit, 1] = imag

    def both_halves(state):
        return [split(jnp.concatenate([state[0, part], state[1, part]], axis=-1)) for part in range(2)]

    def pair(ref):
        return [split(ref[0]), split(ref[1])]

    loads[0].wait()
    prepare(0)
    loads[1].wait()
    values = [split(x[0, 0]), split(x[1, 0])]
    swap0, keep = natural_gate(0, 0, values, send_a, state_a)
    keep()
    loads[2].wait()
    prepare(1)
    loads[3].wait()
    values = [split(x[0, 1]), split(x[1, 1])]
    turned1[...] = interleave(*complex_product(gate(1), values, NT))

    pl.semaphore_wait(barrier, n_wide - 1 + len(partners))
    swap0.start()
    group(1, turned1, got1)

    loads[4].wait()
    prepare(2)
    loads[5].wait()
    prepare(3)

    swap0.wait_recv()
    swap1, keep = natural_gate(2, 1, pair(state_a), send_b, state_b)
    swap1.start()
    keep()
    swap1.wait_recv()
    turned0[...] = interleave(*complex_product(gate(1), pair(state_b), NT))
    group(0, turned0, got0)

    moved1 = group_wait(1, turned1, got1)
    moved1.wait_recv()
    values = [split(part) for part in deinterleave(got1[...])]
    swap2, keep = turned_gate(0, 0, values, tsend_a, tstate_a)
    swap2.start()
    keep()
    swap2.wait_recv()
    swap3, keep = turned_gate(2, 1, both_halves(tstate_a), tsend_b, tstate_b)
    swap3.start()
    keep()
    swap3.wait_recv()
    result[0, 1], result[1, 1] = complex_product(gate(3), both_halves(tstate_b), NT)
    store1 = pltpu.make_async_copy(result.at[:, 1], out_hbm.at[:, 1], out_sem.at[1])
    store1.start()

    moved0 = group_wait(0, turned0, got0)
    moved0.wait_recv()
    values = [split(part) for part in deinterleave(got0[...])]
    result[0, 0], result[1, 0] = complex_product(gate(3), values, NT)
    store0 = pltpu.make_async_copy(result.at[:, 0], out_hbm.at[:, 0], out_sem.at[0])
    store0.start()

    for copy in (swap0, swap1, swap2, swap3, moved1, moved0):
        copy.wait_send()
    store1.wait()
    store0.wait()


def solution(mesh):
    n_narrow, n_wide = mesh.shape["narrow"], mesh.shape["wide"]

    def shards(amplitudes, first_gate, second_gate, swap_gates):
        block = amplitudes.shape[2:]
        reg = block[-1]
        half = reg // 2
        vmem = lambda *shape: pltpu.VMEM(shape, F32)
        out = pl.pallas_call(
            functools.partial(kernel, n_narrow, n_wide),
            out_shape=jax.ShapeDtypeStruct(block, F32),
            in_specs=[pl.BlockSpec(memory_space=pl.ANY)] * 4,
            out_specs=pl.BlockSpec(memory_space=pl.ANY),
            scratch_shapes=[
                vmem(*block),
                vmem(4, 2, reg, reg),
                pltpu.VMEM((4, 2, 2, reg, reg), BF16),
                vmem(2, half, reg),
                vmem(2, reg, reg),
                vmem(2, half, reg),
                vmem(2, reg, reg),
                vmem(2 * reg, reg),
                vmem(2 * reg, reg),
                vmem(2 * reg, reg),
                vmem(2 * reg, reg),
                vmem(2, reg, half),
                vmem(2, 2, reg, half),
                vmem(2, reg, half),
                vmem(2, 2, reg, half),
                vmem(*block),
                pltpu.SemaphoreType.DMA((6,)),
                pltpu.SemaphoreType.DMA((2,)),
                pltpu.SemaphoreType.DMA((4,)),
                pltpu.SemaphoreType.DMA((4,)),
                pltpu.SemaphoreType.DMA((2,)),
                pltpu.SemaphoreType.DMA((2,)),
            ],
            compiler_params=pltpu.CompilerParams(
                collective_id=0, has_side_effects=True, vmem_limit_bytes=40 * 2**20),
            cost_estimate=pl.CostEstimate(flops=8 * 2**30 // 2, bytes_accessed=4 * 2**20, transcendentals=0),
        )(amplitudes[0, 0], first_gate, second_gate, swap_gates)
        return out[None, None]

    return jax.shard_map(
        shards,
        mesh=mesh,
        in_specs=(P("narrow", "wide", None, None, None, None), P(), P(), P()),
        out_specs=P("narrow", "wide", None, None, None, None),
        check_vma=False,
    )
```

```python
import functools

import jax
import jax.numpy as jnp
from jax import lax
from jax.experimental import pallas as pl
from jax.experimental.pallas import tpu as pltpu
from jax.sharding import PartitionSpec as P

MESH = pl.DeviceIdType.MESH
F32 = jnp.float32
BF16 = jnp.bfloat16
PARTS = (4, 4)
PIECES = 2
NN = (((1,), (0,)), ((), ()))
NT = (((1,), (1,)), ((), ()))


def split(x):
    high = x.astype(BF16)
    return high, (x - high.astype(F32)).astype(BF16)


def product(left, right, dims):
    dot = functools.partial(lax.dot_general, dimension_numbers=dims, preferred_element_type=F32)
    return dot(left[0], right[0]) + (dot(left[0], right[1]) + dot(left[1], right[0]))


def complex_product(left, right, dims):
    real = product(left[0], right[0], dims) - product(left[1], right[1], dims)
    imag = product(left[0], right[1], dims) + product(left[1], right[0], dims)
    return real, imag


def top_rows(shape):
    return lax.broadcasted_iota(jnp.int32, shape, 1) < 4


def interleave(real, imag):
    a = real.reshape(-1, 8, real.shape[-1])
    b = imag.reshape(-1, 8, imag.shape[-1])
    top = top_rows(a.shape)
    even = jnp.where(top, a, pltpu.roll(b, 4, 1))
    odd = jnp.where(top, pltpu.roll(a, 4, 1), b)
    return jnp.stack([even, odd], axis=1).reshape(-1, real.shape[-1])


def deinterleave(both):
    pairs = both.reshape(-1, 2, 8, both.shape[-1])
    even, odd = pairs[:, 0], pairs[:, 1]
    top = top_rows(even.shape)
    real = jnp.where(top, even, pltpu.roll(odd, 4, 1))
    imag = jnp.where(top, pltpu.roll(even, 4, 1), odd)
    return real.reshape(-1, both.shape[-1]), imag.reshape(-1, both.shape[-1])


def kernel(n_narrow, n_wide, x_hbm, g1_hbm, g2_hbm, gs_hbm, out_hbm,
           x, gates, split_gates, send_a, state_a, send_b, state_b, turned0, got0,
           turned1, got1, tsend_a, tstate_a, tsend_b, tstate_b, result,
           in_sem, out_sem, swap_send, swap_recv, group_send, group_recv):
    n = lax.axis_index("narrow")
    w = lax.axis_index("wide")
    reg = x.shape[-1]
    half = reg // 2
    top_bit = n_narrow.bit_length() - 2
    bits = (lax.rem(n, 2), lax.rem(n // 2**top_bit, 2))
    partners = (n + 1 - 2 * bits[0], n + (1 - 2 * bits[1]) * 2**top_bit)

    loads = [
        pltpu.make_async_copy(g1_hbm, gates.at[0], in_sem.at[0]),
        pltpu.make_async_copy(x_hbm.at[:, 0], x.at[:, 0], in_sem.at[1]),
        pltpu.make_async_copy(g2_hbm, gates.at[1], in_sem.at[2]),
        pltpu.make_async_copy(x_hbm.at[:, 1], x.at[:, 1], in_sem.at[3]),
        pltpu.make_async_copy(gs_hbm.at[0], gates.at[2], in_sem.at[4]),
        pltpu.make_async_copy(gs_hbm.at[1], gates.at[3], in_sem.at[5]),
    ]
    for load in loads:
        load.start()

    barrier = pltpu.get_barrier_semaphore()
    for partner in partners:
        pl.semaphore_signal(barrier, inc=1, device_id=(partner, w), device_id_type=MESH)

    @pl.loop(1, n_wide)
    def _(k):
        pl.semaphore_signal(barrier, inc=1, device_id=(n, lax.rem(w + k, n_wide)), device_id_type=MESH)

    def prepare(index):
        for part in range(2):
            split_gates[index, part, 0], split_gates[index, part, 1] = split(gates[index, part])

    def gate(index, rows=slice(None)):
        return [(split_gates[index, part, 0, rows, :], split_gates[index, part, 1, rows, :]) for part in range(2)]

    def swap(number, slot, source, target):
        return pltpu.make_async_remote_copy(
            src_ref=source, dst_ref=target, send_sem=swap_send.at[slot], recv_sem=swap_recv.at[slot],
            device_id=(partners[number], w), device_id_type=MESH)

    def group(slot, source, target):
        size = n_wide // PARTS[slot]

        @pl.loop(0, n_wide)
        def _(k):
            other = k // size * size + lax.rem(w + k, size)

            @pl.when(other != w)
            def _():
                pltpu.make_async_remote_copy(
                    src_ref=source.at[pl.ds(pl.multiple_of(other * 8, 8), 8)],
                    dst_ref=target.at[pl.ds(pl.multiple_of(w * 8, 8), 8)],
                    send_sem=group_send.at[slot], recv_sem=group_recv.at[slot],
                    device_id=(n, other), device_id_type=MESH).start()
        own = pl.ds(pl.multiple_of(w * 8, 8), 8)
        target[own, :] = source[own, :]

    def group_wait(slot, source, target):
        moved = pl.ds(0, 8 * (n_wide - 1))
        whole = pltpu.make_async_remote_copy(
            src_ref=source.at[moved], dst_ref=target.at[moved],
            send_sem=group_send.at[slot], recv_sem=group_recv.at[slot],
            device_id=(n, lax.rem(w + 1, n_wide)), device_id_type=MESH)
        return whole

    def rows_of(bit):
        return pl.ds(pl.multiple_of(bit * half, half), half)

    def natural_gate(index, number, values, send, state):
        bit = bits[number]
        send[0], send[1] = complex_product(gate(index, rows_of(1 - bit)), values, NN)
        copy = swap(number, number, send, state.at[:, rows_of(bit), :])
        keep = functools.partial(keep_natural, index, bit, values, state)
        return copy, keep

    def keep_natural(index, bit, values, state):
        real, imag = complex_product(gate(index, rows_of(bit)), values, NN)
        state[0, rows_of(bit), :] = real
        state[1, rows_of(bit), :] = imag

    def turned_gate(index, number, piece, values, send, state):
        bit = bits[number]
        send[piece, 0], send[piece, 1] = complex_product(values, gate(index, rows_of(1 - bit)), NT)
        copy = swap(number, 2 + 2 * piece + number, send.at[piece], state.at[piece, bit])
        copy.start()
        real, imag = complex_product(values, gate(index, rows_of(bit)), NT)
        state[piece, bit, 0] = real
        state[piece, bit, 1] = imag
        return copy

    def both_halves(state, piece):
        return [split(jnp.concatenate([state[piece, 0, part], state[piece, 1, part]], axis=-1)) for part in range(2)]

    def pair(ref):
        return [split(ref[0]), split(ref[1])]

    loads[0].wait()
    prepare(0)
    loads[1].wait()
    values = [split(x[0, 0]), split(x[1, 0])]
    swap0, keep = natural_gate(0, 0, values, send_a, state_a)
    keep()
    loads[2].wait()
    prepare(1)
    loads[3].wait()
    values = [split(x[0, 1]), split(x[1, 1])]
    turned1[...] = interleave(*complex_product(gate(1), values, NT))

    pl.semaphore_wait(barrier, n_wide - 1 + len(partners))
    swap0.start()
    group(1, turned1, got1)

    loads[4].wait()
    prepare(2)
    loads[5].wait()
    prepare(3)

    swap0.wait_recv()
    swap1, keep = natural_gate(2, 1, pair(state_a), send_b, state_b)
    swap1.start()
    keep()
    swap1.wait_recv()
    turned0[...] = interleave(*complex_product(gate(1), pair(state_b), NT))
    group(0, turned0, got0)

    moved1 = group_wait(1, turned1, got1)
    moved1.wait_recv()
    swaps2, swaps3 = [], []
    for piece in range(PIECES):
        values = [split(part) for part in deinterleave(got1[piece * reg:(piece + 1) * reg, :])]
        swaps2.append(turned_gate(0, 0, piece, values, tsend_a, tstate_a))
    for piece in range(PIECES):
        swaps2[piece].wait_recv()
        swaps3.append(turned_gate(2, 1, piece, both_halves(tstate_a, piece), tsend_b, tstate_b))
    for piece in range(PIECES):
        swaps3[piece].wait_recv()
        columns = slice(piece * half, (piece + 1) * half)
        result[0, 1, :, columns], result[1, 1, :, columns] = complex_product(gate(3), both_halves(tstate_b, piece), NT)
    store1 = pltpu.make_async_copy(result.at[:, 1], out_hbm.at[:, 1], out_sem.at[1])
    store1.start()

    moved0 = group_wait(0, turned0, got0)
    moved0.wait_recv()
    values = [split(part) for part in deinterleave(got0[...])]
    result[0, 0], result[1, 0] = complex_product(gate(3), values, NT)
    store0 = pltpu.make_async_copy(result.at[:, 0], out_hbm.at[:, 0], out_sem.at[0])
    store0.start()

    for copy in (swap0, swap1, *swaps2, *swaps3, moved1, moved0):
        copy.wait_send()
    store1.wait()
    store0.wait()


def solution(mesh):
    n_narrow, n_wide = mesh.shape["narrow"], mesh.shape["wide"]

    def shards(amplitudes, first_gate, second_gate, swap_gates):
        block = amplitudes.shape[2:]
        reg = block[-1]
        half = reg // 2
        vmem = lambda *shape: pltpu.VMEM(shape, F32)
        out = pl.pallas_call(
            functools.partial(kernel, n_narrow, n_wide),
            out_shape=jax.ShapeDtypeStruct(block, F32),
            in_specs=[pl.BlockSpec(memory_space=pl.ANY)] * 4,
            out_specs=pl.BlockSpec(memory_space=pl.ANY),
            scratch_shapes=[
                vmem(*block),
                vmem(4, 2, reg, reg),
                pltpu.VMEM((4, 2, 2, reg, reg), BF16),
                vmem(2, half, reg),
                vmem(2, reg, reg),
                vmem(2, half, reg),
                vmem(2, reg, reg),
                vmem(2 * reg, reg),
                vmem(2 * reg, reg),
                vmem(2 * reg, reg),
                vmem(2 * reg, reg),
                vmem(PIECES, 2, reg // PIECES, half),
                vmem(PIECES, 2, 2, reg // PIECES, half),
                vmem(PIECES, 2, reg // PIECES, half),
                vmem(PIECES, 2, 2, reg // PIECES, half),
                vmem(*block),
                pltpu.SemaphoreType.DMA((6,)),
                pltpu.SemaphoreType.DMA((2,)),
                pltpu.SemaphoreType.DMA((2 + 2 * PIECES,)),
                pltpu.SemaphoreType.DMA((2 + 2 * PIECES,)),
                pltpu.SemaphoreType.DMA((2,)),
                pltpu.SemaphoreType.DMA((2,)),
            ],
            compiler_params=pltpu.CompilerParams(
                collective_id=0, has_side_effects=True, vmem_limit_bytes=60 * 2**20),
            cost_estimate=pl.CostEstimate(flops=8 * 2**30 // 2, bytes_accessed=4 * 2**20, transcendentals=0),
        )(amplitudes[0, 0], first_gate, second_gate, swap_gates)
        return out[None, None]

    return jax.shard_map(
        shards,
        mesh=mesh,
        in_specs=(P("narrow", "wide", None, None, None, None), P(), P(), P()),
        out_specs=P("narrow", "wide", None, None, None, None),
        check_vma=False,
    )
```

```python
import functools

import jax
import jax.numpy as jnp
from jax import lax
from jax.experimental import pallas as pl
from jax.experimental.pallas import tpu as pltpu
from jax.sharding import PartitionSpec as P

MESH = pl.DeviceIdType.MESH
F32 = jnp.float32
BF16 = jnp.bfloat16
ORDER = ((0, 0), (1, 0), (0, 1), (2, 0), (1, 1), (3, 0), (2, 1), (3, 1))
PIECES = 2
NN = (((1,), (0,)), ((), ()))
NT = (((1,), (1,)), ((), ()))


def split(x):
    high = x.astype(BF16)
    return high, (x - high.astype(F32)).astype(BF16)


def product(left, right, dims):
    dot = functools.partial(lax.dot_general, dimension_numbers=dims, preferred_element_type=F32)
    return dot(left[0], right[0]) + (dot(left[0], right[1]) + dot(left[1], right[0]))


def complex_product(left, right, dims):
    real = product(left[0], right[0], dims) - product(left[1], right[1], dims)
    imag = product(left[0], right[1], dims) + product(left[1], right[0], dims)
    return real, imag


def top_rows(shape):
    return lax.broadcasted_iota(jnp.int32, shape, 1) < 4


def interleave(real, imag):
    a = real.reshape(-1, 8, real.shape[-1])
    b = imag.reshape(-1, 8, imag.shape[-1])
    top = top_rows(a.shape)
    even = jnp.where(top, a, pltpu.roll(b, 4, 1))
    odd = jnp.where(top, pltpu.roll(a, 4, 1), b)
    return jnp.stack([even, odd], axis=1).reshape(-1, real.shape[-1])


def deinterleave(both):
    pairs = both.reshape(-1, 2, 8, both.shape[-1])
    even, odd = pairs[:, 0], pairs[:, 1]
    top = top_rows(even.shape)
    real = jnp.where(top, even, pltpu.roll(odd, 4, 1))
    imag = jnp.where(top, pltpu.roll(even, 4, 1), odd)
    return real.reshape(-1, both.shape[-1]), imag.reshape(-1, both.shape[-1])


def kernel(n_narrow, n_wide, x_hbm, g1_hbm, g2_hbm, gs_hbm, out_hbm,
           x, gates, split_gates, send_a, state_a, send_b, state_b, turned0, got0,
           turned1, got1, tsend_a, tstate_a, tsend_b, tstate_b, result,
           in_sem, out_sem, swap_send, swap_recv, group_send, group_recv):
    n = lax.axis_index("narrow")
    w = lax.axis_index("wide")
    reg = x.shape[-1]
    half = reg // 2
    top_bit = n_narrow.bit_length() - 2
    bits = (lax.rem(n, 2), lax.rem(n // 2**top_bit, 2))
    partners = (n + 1 - 2 * bits[0], n + (1 - 2 * bits[1]) * 2**top_bit)

    loads = [
        pltpu.make_async_copy(g1_hbm, gates.at[0], in_sem.at[0]),
        pltpu.make_async_copy(x_hbm.at[:, 0], x.at[:, 0], in_sem.at[1]),
        pltpu.make_async_copy(g2_hbm, gates.at[1], in_sem.at[2]),
        pltpu.make_async_copy(x_hbm.at[:, 1], x.at[:, 1], in_sem.at[3]),
        pltpu.make_async_copy(gs_hbm.at[0], gates.at[2], in_sem.at[4]),
        pltpu.make_async_copy(gs_hbm.at[1], gates.at[3], in_sem.at[5]),
    ]
    for load in loads:
        load.start()

    barrier = pltpu.get_barrier_semaphore()
    for partner in partners:
        pl.semaphore_signal(barrier, inc=1, device_id=(partner, w), device_id_type=MESH)

    @pl.loop(1, n_wide)
    def _(k):
        pl.semaphore_signal(barrier, inc=1, device_id=(n, lax.rem(w + k, n_wide)), device_id_type=MESH)

    def prepare(index):
        for part in range(2):
            split_gates[index, part, 0], split_gates[index, part, 1] = split(gates[index, part])

    def gate(index, rows=slice(None)):
        return [(split_gates[index, part, 0, rows, :], split_gates[index, part, 1, rows, :]) for part in range(2)]

    def swap(number, slot, source, target):
        return pltpu.make_async_remote_copy(
            src_ref=source, dst_ref=target, send_sem=swap_send.at[slot], recv_sem=swap_recv.at[slot],
            device_id=(partners[number], w), device_id_type=MESH)

    def group(slot, source, target):
        run = n_wide // 8

        for quarter, middle in ORDER:
            @pl.loop(0, run)
            def _(k):
                place = lax.rem(w // 4 * 2 + lax.rem(w, 2) + k, run)
                other = quarter * 2 * run + place // 2 * 4 + middle * 2 + lax.rem(place, 2)

                @pl.when(other != w)
                def _():
                    pltpu.make_async_remote_copy(
                        src_ref=source.at[pl.ds(pl.multiple_of(other * 8, 8), 8)],
                        dst_ref=target.at[pl.ds(pl.multiple_of(w * 8, 8), 8)],
                        send_sem=group_send.at[slot], recv_sem=group_recv.at[slot],
                        device_id=(n, other), device_id_type=MESH).start()
        own = pl.ds(pl.multiple_of(w * 8, 8), 8)
        target[own, :] = source[own, :]

    def group_wait(slot, source, target):
        moved = pl.ds(0, 8 * (n_wide - 1))
        whole = pltpu.make_async_remote_copy(
            src_ref=source.at[moved], dst_ref=target.at[moved],
            send_sem=group_send.at[slot], recv_sem=group_recv.at[slot],
            device_id=(n, lax.rem(w + 1, n_wide)), device_id_type=MESH)
        return whole

    def rows_of(bit):
        return pl.ds(pl.multiple_of(bit * half, half), half)

    def natural_gate(index, number, piece, values, send, state):
        bit = bits[number]
        send[piece, 0], send[piece, 1] = complex_product(gate(index, rows_of(1 - bit)), values, NN)
        copy = swap(number, 2 * piece + number, send.at[piece], state.at[piece, :, rows_of(bit), :])
        return copy, functools.partial(keep_natural, index, bit, piece, values, state)

    def keep_natural(index, bit, piece, values, state):
        real, imag = complex_product(gate(index, rows_of(bit)), values, NN)
        state[piece, 0, rows_of(bit), :] = real
        state[piece, 1, rows_of(bit), :] = imag

    def turned_gate(index, number, piece, values, send, state):
        bit = bits[number]
        send[piece, 0], send[piece, 1] = complex_product(values, gate(index, rows_of(1 - bit)), NT)
        copy = swap(number, 2 * PIECES + 2 * piece + number, send.at[piece], state.at[piece, bit])
        copy.start()
        real, imag = complex_product(values, gate(index, rows_of(bit)), NT)
        state[piece, bit, 0] = real
        state[piece, bit, 1] = imag
        return copy

    def both_halves(state, piece):
        return [split(jnp.concatenate([state[piece, 0, part], state[piece, 1, part]], axis=-1)) for part in range(2)]

    def columns(piece):
        return slice(piece * reg // PIECES, (piece + 1) * reg // PIECES)

    loads[0].wait()
    prepare(0)
    loads[1].wait()
    swaps0, swaps1 = [], []
    for piece in range(PIECES):
        values = [split(x[part, 0, :, columns(piece)]) for part in range(2)]
        copy, keep = natural_gate(0, 0, piece, values, send_a, state_a)
        keep()
        swaps0.append(copy)
    loads[2].wait()
    prepare(1)
    loads[3].wait()
    values = [split(x[0, 1]), split(x[1, 1])]
    turned1[...] = interleave(*complex_product(gate(1), values, NT))

    pl.semaphore_wait(barrier, n_wide - 1 + len(partners))
    for copy in swaps0:
        copy.start()
    group(1, turned1, got1)

    loads[4].wait()
    prepare(2)
    loads[5].wait()
    prepare(3)

    for piece in range(PIECES):
        swaps0[piece].wait_recv()
        values = [split(state_a[piece, part]) for part in range(2)]
        copy, keep = natural_gate(2, 1, piece, values, send_b, state_b)
        copy.start()
        keep()
        swaps1.append(copy)
    for copy in swaps1:
        copy.wait_recv()
    values = [split(jnp.concatenate([state_b[piece, part] for piece in range(PIECES)], axis=-1)) for part in range(2)]
    turned0[...] = interleave(*complex_product(gate(1), values, NT))
    group(0, turned0, got0)

    moved1 = group_wait(1, turned1, got1)
    moved1.wait_recv()
    swaps2, swaps3 = [], []
    for piece in range(PIECES):
        values = [split(part) for part in deinterleave(got1[piece * reg:(piece + 1) * reg, :])]
        swaps2.append(turned_gate(0, 0, piece, values, tsend_a, tstate_a))
    for piece in range(PIECES):
        swaps2[piece].wait_recv()
        swaps3.append(turned_gate(2, 1, piece, both_halves(tstate_a, piece), tsend_b, tstate_b))
    for piece in range(PIECES):
        swaps3[piece].wait_recv()
        result[0, 1, :, columns(piece)], result[1, 1, :, columns(piece)] = complex_product(gate(3), both_halves(tstate_b, piece), NT)
    store1 = pltpu.make_async_copy(result.at[:, 1], out_hbm.at[:, 1], out_sem.at[1])
    store1.start()

    moved0 = group_wait(0, turned0, got0)
    moved0.wait_recv()
    values = [split(part) for part in deinterleave(got0[...])]
    result[0, 0], result[1, 0] = complex_product(gate(3), values, NT)
    store0 = pltpu.make_async_copy(result.at[:, 0], out_hbm.at[:, 0], out_sem.at[0])
    store0.start()

    for copy in (*swaps0, *swaps1, *swaps2, *swaps3, moved1, moved0):
        copy.wait_send()
    store1.wait()
    store0.wait()


def solution(mesh):
    n_narrow, n_wide = mesh.shape["narrow"], mesh.shape["wide"]

    def shards(amplitudes, first_gate, second_gate, swap_gates):
        block = amplitudes.shape[2:]
        reg = block[-1]
        half = reg // 2
        vmem = lambda *shape: pltpu.VMEM(shape, F32)
        out = pl.pallas_call(
            functools.partial(kernel, n_narrow, n_wide),
            out_shape=jax.ShapeDtypeStruct(block, F32),
            in_specs=[pl.BlockSpec(memory_space=pl.ANY)] * 4,
            out_specs=pl.BlockSpec(memory_space=pl.ANY),
            scratch_shapes=[
                vmem(*block),
                vmem(4, 2, reg, reg),
                pltpu.VMEM((4, 2, 2, reg, reg), BF16),
                vmem(PIECES, 2, half, reg // PIECES),
                vmem(PIECES, 2, reg, reg // PIECES),
                vmem(PIECES, 2, half, reg // PIECES),
                vmem(PIECES, 2, reg, reg // PIECES),
                vmem(2 * reg, reg),
                vmem(2 * reg, reg),
                vmem(2 * reg, reg),
                vmem(2 * reg, reg),
                vmem(PIECES, 2, reg // PIECES, half),
                vmem(PIECES, 2, 2, reg // PIECES, half),
                vmem(PIECES, 2, reg // PIECES, half),
                vmem(PIECES, 2, 2, reg // PIECES, half),
                vmem(*block),
                pltpu.SemaphoreType.DMA((6,)),
                pltpu.SemaphoreType.DMA((2,)),
                pltpu.SemaphoreType.DMA((4 * PIECES,)),
                pltpu.SemaphoreType.DMA((4 * PIECES,)),
                pltpu.SemaphoreType.DMA((2,)),
                pltpu.SemaphoreType.DMA((2,)),
            ],
            compiler_params=pltpu.CompilerParams(
                collective_id=0, has_side_effects=True, vmem_limit_bytes=60 * 2**20),
            cost_estimate=pl.CostEstimate(flops=8 * 2**30 // 2, bytes_accessed=4 * 2**20, transcendentals=0),
        )(amplitudes[0, 0], first_gate, second_gate, swap_gates)
        return out[None, None]

    return jax.shard_map(
        shards,
        mesh=mesh,
        in_specs=(P("narrow", "wide", None, None, None, None), P(), P(), P()),
        out_specs=P("narrow", "wide", None, None, None, None),
        check_vma=False,
    )
```

```python
import functools

import jax
import jax.numpy as jnp
from jax import lax
from jax.experimental import pallas as pl
from jax.experimental.pallas import tpu as pltpu
from jax.sharding import PartitionSpec as P

MESH = pl.DeviceIdType.MESH
F32 = jnp.float32
BF16 = jnp.bfloat16
ORDER = ((0, 0), (1, 0), (0, 1), (2, 0), (1, 1), (3, 0), (2, 1), (3, 1))
PIECES = 2
FINER = 4
NN = (((1,), (0,)), ((), ()))
NT = (((1,), (1,)), ((), ()))


def split(x):
    high = x.astype(BF16)
    return high, (x - high.astype(F32)).astype(BF16)


def product(left, right, dims):
    dot = functools.partial(lax.dot_general, dimension_numbers=dims, preferred_element_type=F32)
    return dot(left[0], right[0]) + (dot(left[0], right[1]) + dot(left[1], right[0]))


def complex_product(left, right, dims):
    real = product(left[0], right[0], dims) - product(left[1], right[1], dims)
    imag = product(left[0], right[1], dims) + product(left[1], right[0], dims)
    return real, imag


def top_rows(shape):
    return lax.broadcasted_iota(jnp.int32, shape, 1) < 4


def interleave(real, imag):
    a = real.reshape(-1, 8, real.shape[-1])
    b = imag.reshape(-1, 8, imag.shape[-1])
    top = top_rows(a.shape)
    even = jnp.where(top, a, pltpu.roll(b, 4, 1))
    odd = jnp.where(top, pltpu.roll(a, 4, 1), b)
    return jnp.stack([even, odd], axis=1).reshape(-1, real.shape[-1])


def deinterleave(both):
    pairs = both.reshape(-1, 2, 8, both.shape[-1])
    even, odd = pairs[:, 0], pairs[:, 1]
    top = top_rows(even.shape)
    real = jnp.where(top, even, pltpu.roll(odd, 4, 1))
    imag = jnp.where(top, pltpu.roll(even, 4, 1), odd)
    return real.reshape(-1, both.shape[-1]), imag.reshape(-1, both.shape[-1])


def kernel(n_narrow, n_wide, x_hbm, g1_hbm, g2_hbm, gs_hbm, out_hbm,
           x, gates, split_gates, send_a, state_a, send_b, state_b, turned0, got0,
           turned1, got1, tsend_a, tstate_a, tsend_b, tstate_b, result,
           in_sem, out_sem, swap_send, swap_recv, group_send, group_recv):
    n = lax.axis_index("narrow")
    w = lax.axis_index("wide")
    reg = x.shape[-1]
    half = reg // 2
    top_bit = n_narrow.bit_length() - 2
    bits = (lax.rem(n, 2), lax.rem(n // 2**top_bit, 2))
    partners = (n + 1 - 2 * bits[0], n + (1 - 2 * bits[1]) * 2**top_bit)

    loads = [
        pltpu.make_async_copy(g1_hbm, gates.at[0], in_sem.at[0]),
        pltpu.make_async_copy(x_hbm.at[:, 0], x.at[:, 0], in_sem.at[1]),
        pltpu.make_async_copy(g2_hbm, gates.at[1], in_sem.at[2]),
        pltpu.make_async_copy(x_hbm.at[:, 1], x.at[:, 1], in_sem.at[3]),
        pltpu.make_async_copy(gs_hbm.at[0], gates.at[2], in_sem.at[4]),
        pltpu.make_async_copy(gs_hbm.at[1], gates.at[3], in_sem.at[5]),
    ]
    for load in loads:
        load.start()

    barrier = pltpu.get_barrier_semaphore()
    for partner in partners:
        pl.semaphore_signal(barrier, inc=1, device_id=(partner, w), device_id_type=MESH)

    @pl.loop(1, n_wide)
    def _(k):
        pl.semaphore_signal(barrier, inc=1, device_id=(n, lax.rem(w + k, n_wide)), device_id_type=MESH)

    def prepare(index):
        for part in range(2):
            split_gates[index, part, 0], split_gates[index, part, 1] = split(gates[index, part])

    def gate(index, rows=slice(None)):
        return [(split_gates[index, part, 0, rows, :], split_gates[index, part, 1, rows, :]) for part in range(2)]

    def swap(number, slot, source, target):
        return pltpu.make_async_remote_copy(
            src_ref=source, dst_ref=target, send_sem=swap_send.at[slot], recv_sem=swap_recv.at[slot],
            device_id=(partners[number], w), device_id_type=MESH)

    def group(slot, source, target):
        run = n_wide // 8

        for quarter, middle in ORDER:
            @pl.loop(0, run)
            def _(k):
                place = lax.rem(w // 4 * 2 + lax.rem(w, 2) + k, run)
                other = quarter * 2 * run + place // 2 * 4 + middle * 2 + lax.rem(place, 2)

                @pl.when(other != w)
                def _():
                    pltpu.make_async_remote_copy(
                        src_ref=source.at[pl.ds(pl.multiple_of(other * 8, 8), 8)],
                        dst_ref=target.at[pl.ds(pl.multiple_of(w * 8, 8), 8)],
                        send_sem=group_send.at[slot], recv_sem=group_recv.at[slot],
                        device_id=(n, other), device_id_type=MESH).start()
        own = pl.ds(pl.multiple_of(w * 8, 8), 8)
        target[own, :] = source[own, :]

    def group_wait(slot, source, target):
        moved = pl.ds(0, 8 * (n_wide - 1))
        whole = pltpu.make_async_remote_copy(
            src_ref=source.at[moved], dst_ref=target.at[moved],
            send_sem=group_send.at[slot], recv_sem=group_recv.at[slot],
            device_id=(n, lax.rem(w + 1, n_wide)), device_id_type=MESH)
        return whole

    def rows_of(bit):
        return pl.ds(pl.multiple_of(bit * half, half), half)

    def natural_gate(index, number, piece, values, send, state):
        bit = bits[number]
        send[piece, 0], send[piece, 1] = complex_product(gate(index, rows_of(1 - bit)), values, NN)
        copy = swap(number, 2 * piece + number, send.at[piece], state.at[piece, :, rows_of(bit), :])
        return copy, functools.partial(keep_natural, index, bit, piece, values, state)

    def keep_natural(index, bit, piece, values, state):
        real, imag = complex_product(gate(index, rows_of(bit)), values, NN)
        state[piece, 0, rows_of(bit), :] = real
        state[piece, 1, rows_of(bit), :] = imag

    def turned_gate(index, number, piece, values, send, state):
        bit = bits[number]
        send[piece, 0], send[piece, 1] = complex_product(values, gate(index, rows_of(1 - bit)), NT)
        copy = swap(number, 2 * PIECES + 2 * piece + number, send.at[piece], state.at[piece, bit])
        copy.start()
        real, imag = complex_product(values, gate(index, rows_of(bit)), NT)
        state[piece, bit, 0] = real
        state[piece, bit, 1] = imag
        return copy

    def both_halves(state, pieces):
        rows = [[jnp.concatenate([state[piece, 0, part], state[piece, 1, part]], axis=-1) for piece in pieces] for part in range(2)]
        return [split(jnp.concatenate(of_part, axis=0)) for of_part in rows]

    def columns(piece):
        return slice(piece * reg // PIECES, (piece + 1) * reg // PIECES)

    loads[0].wait()
    prepare(0)
    loads[1].wait()
    swaps0, swaps1 = [], []
    for piece in range(PIECES):
        values = [split(x[part, 0, :, columns(piece)]) for part in range(2)]
        copy, keep = natural_gate(0, 0, piece, values, send_a, state_a)
        keep()
        swaps0.append(copy)
    loads[2].wait()
    prepare(1)
    loads[3].wait()
    values = [split(x[0, 1]), split(x[1, 1])]
    turned1[...] = interleave(*complex_product(gate(1), values, NT))

    pl.semaphore_wait(barrier, n_wide - 1 + len(partners))
    for copy in swaps0:
        copy.start()
    group(1, turned1, got1)

    loads[4].wait()
    prepare(2)
    loads[5].wait()
    prepare(3)

    for piece in range(PIECES):
        swaps0[piece].wait_recv()
        values = [split(state_a[piece, part]) for part in range(2)]
        copy, keep = natural_gate(2, 1, piece, values, send_b, state_b)
        copy.start()
        keep()
        swaps1.append(copy)
    for copy in swaps1:
        copy.wait_recv()
    values = [split(jnp.concatenate([state_b[piece, part] for piece in range(PIECES)], axis=-1)) for part in range(2)]
    turned0[...] = interleave(*complex_product(gate(1), values, NT))
    group(0, turned0, got0)

    moved1 = group_wait(1, turned1, got1)
    moved1.wait_recv()
    swaps2, swaps3 = [], []
    tall = 2 * reg // FINER
    for piece in range(FINER):
        values = [split(part) for part in deinterleave(got1[piece * tall:(piece + 1) * tall, :])]
        swaps2.append(turned_gate(0, 0, piece, values, tsend_a, tstate_a))
    for piece in range(FINER):
        swaps2[piece].wait_recv()
        swaps3.append(turned_gate(2, 1, piece, both_halves(tstate_a, [piece]), tsend_b, tstate_b))
    for piece in range(PIECES):
        parts = range(piece * FINER // PIECES, (piece + 1) * FINER // PIECES)
        for part in parts:
            swaps3[part].wait_recv()
        result[0, 1, :, columns(piece)], result[1, 1, :, columns(piece)] = complex_product(gate(3), both_halves(tstate_b, parts), NT)
    store1 = pltpu.make_async_copy(result.at[:, 1], out_hbm.at[:, 1], out_sem.at[1])
    store1.start()

    moved0 = group_wait(0, turned0, got0)
    moved0.wait_recv()
    values = [split(part) for part in deinterleave(got0[...])]
    result[0, 0], result[1, 0] = complex_product(gate(3), values, NT)
    store0 = pltpu.make_async_copy(result.at[:, 0], out_hbm.at[:, 0], out_sem.at[0])
    store0.start()

    for copy in (*swaps0, *swaps1, *swaps2, *swaps3, moved1, moved0):
        copy.wait_send()
    store1.wait()
    store0.wait()


def solution(mesh):
    n_narrow, n_wide = mesh.shape["narrow"], mesh.shape["wide"]

    def shards(amplitudes, first_gate, second_gate, swap_gates):
        block = amplitudes.shape[2:]
        reg = block[-1]
        half = reg // 2
        vmem = lambda *shape: pltpu.VMEM(shape, F32)
        out = pl.pallas_call(
            functools.partial(kernel, n_narrow, n_wide),
            out_shape=jax.ShapeDtypeStruct(block, F32),
            in_specs=[pl.BlockSpec(memory_space=pl.ANY)] * 4,
            out_specs=pl.BlockSpec(memory_space=pl.ANY),
            scratch_shapes=[
                vmem(*block),
                vmem(4, 2, reg, reg),
                pltpu.VMEM((4, 2, 2, reg, reg), BF16),
                vmem(PIECES, 2, half, reg // PIECES),
                vmem(PIECES, 2, reg, reg // PIECES),
                vmem(PIECES, 2, half, reg // PIECES),
                vmem(PIECES, 2, reg, reg // PIECES),
                vmem(2 * reg, reg),
                vmem(2 * reg, reg),
                vmem(2 * reg, reg),
                vmem(2 * reg, reg),
                vmem(FINER, 2, reg // FINER, half),
                vmem(FINER, 2, 2, reg // FINER, half),
                vmem(FINER, 2, reg // FINER, half),
                vmem(FINER, 2, 2, reg // FINER, half),
                vmem(*block),
                pltpu.SemaphoreType.DMA((6,)),
                pltpu.SemaphoreType.DMA((2,)),
                pltpu.SemaphoreType.DMA((2 * PIECES + 2 * FINER,)),
                pltpu.SemaphoreType.DMA((2 * PIECES + 2 * FINER,)),
                pltpu.SemaphoreType.DMA((2,)),
                pltpu.SemaphoreType.DMA((2,)),
            ],
            compiler_params=pltpu.CompilerParams(
                collective_id=0, has_side_effects=True, vmem_limit_bytes=60 * 2**20),
            cost_estimate=pl.CostEstimate(flops=8 * 2**30 // 2, bytes_accessed=4 * 2**20, transcendentals=0),
        )(amplitudes[0, 0], first_gate, second_gate, swap_gates)
        return out[None, None]

    return jax.shard_map(
        shards,
        mesh=mesh,
        in_specs=(P("narrow", "wide", None, None, None, None), P(), P(), P()),
        out_specs=P("narrow", "wide", None, None, None, None),
        check_vma=False,
    )
```
